512 devices in a mesh: enc: 128 (over x, y_hi, z), dec: 4 (over y_lo, core).
Axes of the slice: x: 4, y: 8 (y_hi: 4, y_lo: 2; y = y_hi * 2 + y_lo), z: 8, core: 2. Of those that a mesh axis runs over, the one named last changes fastest.
Arguments:
- dec_states: bfloat16 [2, 8192, 2048], P(None, 'enc'), may hold values from -24 to 24
- enc_states: bfloat16 [2, 32768, 2048], P(None, 'enc'), may hold values from -144 to 144
- w_query: bfloat16 [2048, 2048], P('enc', 'dec'), may hold values from -0.125 to 0.125
- w_key: bfloat16 [2048, 2048], P('enc', 'dec'), may hold values from -0.125 to 0.125
- w_value: bfloat16 [2048, 2048], P('enc', 'dec'), may hold values from -0.125 to 0.125
- passage_slot: int32 [128, 4], P('enc'), may hold values from 0 to 3, each once within a row
- ctx_grad: bfloat16 [2, 8192, 2048], P(None, 'enc', 'dec'), may hold values from -24 to 24
Outputs:
- context: bfloat16 [2, 8192, 2048], P(None, 'enc', 'dec')
- grad_query: float32 [2048, 2048], P('enc', 'dec')
- grad_enc: bfloat16 [2, 32768, 2048], P(None, 'enc')
The draws below stay inside these ranges and needn't reach their ends.
All inputs are finite; a program needn't handle non-finite values.
Results may differ from the reference program's by a relative error of at most 0.022.
The reference program's roundings to bfloat16 on the way count: a program that leaves them out, or rounds other values in their place, can miss the bound.
Values may be sent and summed in bfloat16 or wider, within the bound.
No kernel may reach another device: no remote copies, remote signals or barrier semaphores. Data moves between devices by JAX's collectives and lax.ppermute only.
A program may use at most 64 MiB of HBM per device.

```python
import math
import jax
import jax.numpy as jnp
from jax import lax

D = 2048
HEADS = 32
HEAD_DIM = 64
PASSAGES = 4
PASS_LEN = 64
TD = 64
MB = 2
INNER = 2048
KEYS = 256
ENC_ROWS = 32768
DEC_ROWS = 8192
N_ENC = 128
N_DEC = 4


def draw_enc_states(key, part):
    key = jax.random.fold_in(key, 7)
    first_key, second_key = jax.random.split(key)
    normals = jnp.clip(jax.random.normal(first_key, (MB, ENC_ROWS, D), jnp.float32), -6.0, 6.0)
    scales = jnp.exp(jax.random.uniform(second_key, (MB, ENC_ROWS, 1), jnp.float32, math.log(0.5), math.log(4.0)))
    return (normals * scales).astype(jnp.bfloat16)


def spiked(entries, stream_key, source, target, shards_of, factor):
    owner, partner = [(jnp.arange(entries.shape[position]) // (entries.shape[position] // shards_of)).reshape([-1 if axis == position else 1 for axis in range(entries.ndim)]) for position in (source, target)]
    chosen = jax.random.permutation(stream_key, shards_of)[partner]
    strong = (owner == chosen) | (owner == (partner + shards_of // 2) % shards_of)
    return jnp.where(strong, factor * entries, entries)


def steps_of(stream_key, dims, shards, low, high):
    def one(dim, parts):
        steps = jax.random.uniform(jax.random.fold_in(jax.random.fold_in(stream_key, 6), dim), (parts,), jnp.float32, low / len(shards), high / len(shards))
        return jnp.repeat(jnp.exp(steps), dims[dim] // parts).reshape((-1,) + (1,) * (len(dims) - dim - 1))

    level = one(*shards[0])
    for cut in shards[1:]:
        level = level * one(*cut)
    return level


def noise(own_key, extent, deviation, most, cuts=(), kind=jnp.bfloat16):
    result = jax.random.normal(own_key, extent, jnp.float32) * deviation
    if len(cuts) > 0:
        result = steps_of(own_key, extent, cuts, -0.22, 0.18) * result
    return jnp.clip(result, min=-most, max=most).astype(kind)


def bell_draw_with(own_key, extent, width, most, pieces, heavy, held_as=jnp.bfloat16):
    array = width * jax.random.normal(own_key, extent, jnp.float32)
    if pieces:
        array = array * steps_of(own_key, extent, pieces, -0.22, 0.18)
    return jnp.clip(spiked(array, jax.random.fold_in(own_key, 3), *heavy), -most, most).astype(held_as)


def setup_inputs(seed: int = 0) -> dict:
    key_list = jax.random.split(jax.random.key(seed), 8)
    return {
        "dec_states": bell_draw_with(key_list[0], (MB, DEC_ROWS, D), 1.0, 24.0, ((1, 128),), (1, 2, 128, 5.5)),
        "enc_states": draw_enc_states(jax.random.fold_in(key_list[7], 71), 0),
        "w_query": noise(key_list[2], (D, INNER), D ** -0.5, 0.125, ((0, 128), (1, 4))),
        "w_key": noise(key_list[3], (D, INNER), D ** -0.5, 0.125, ((0, 128), (1, 4))),
        "w_value": noise(key_list[4], (D, INNER), D ** -0.5, 0.125, ((0, 128), (1, 4))),
        "passage_slot": jax.vmap(lambda own: jax.random.permutation(own, PASSAGES))(jax.random.split(key_list[5], N_ENC)).reshape((N_ENC, PASSAGES)).astype(jnp.int32),
        "ctx_grad": jnp.clip(jax.random.uniform(key_list[6], (MB, DEC_ROWS, INNER), jnp.float32, -24.0, 24.0) * steps_of(key_list[6], (MB, DEC_ROWS, INNER), ((1, 128), (2, 4)), -0.4, 0.0), -24.0, 24.0).astype(jnp.bfloat16),
    }


SCALE = 0.125


def build_index(passage_slot):
    questions = jnp.arange(N_ENC, dtype=jnp.int32)
    offsets = jnp.arange(PASSAGES, dtype=jnp.int32)
    holder = (questions[:, None] + offsets[None, :]) % N_ENC
    slot_index = passage_slot[holder, offsets[None, :]].astype(jnp.int32)
    first_rows = holder * KEYS + slot_index * PASS_LEN
    within = jnp.arange(PASS_LEN, dtype=jnp.int32)
    return (first_rows[:, :, None] + within[None, None, :]).reshape(N_ENC, KEYS).astype(jnp.int32)


def question_pass(items):
    queries, key_rows, value_rows, grad_out = items
    query_heads = queries.reshape(TD, HEADS, HEAD_DIM).astype(jnp.float32)
    key_heads = key_rows.reshape(KEYS, HEADS, HEAD_DIM).astype(jnp.float32)
    value_heads = value_rows.reshape(KEYS, HEADS, HEAD_DIM).astype(jnp.float32)
    grad_heads = grad_out.reshape(TD, HEADS, HEAD_DIM).astype(jnp.float32)
    scores = jnp.einsum("qhd,khd->hqk", query_heads, key_heads) * SCALE
    largest = jnp.max(scores, axis=-1, keepdims=True)
    raw_weights = jnp.exp(scores - largest)
    attention = raw_weights / jnp.sum(raw_weights, axis=-1, keepdims=True)
    attention_low = attention.astype(jnp.bfloat16).astype(jnp.float32)
    context = jnp.einsum("hqk,khd->qhd", attention_low, value_heads).astype(jnp.bfloat16)
    grad_attention = jnp.einsum("qhd,khd->hqk", grad_heads, value_heads)
    correction = jnp.sum(attention * grad_attention, axis=-1, keepdims=True)
    grad_scores = (attention * (grad_attention - correction) * SCALE).astype(jnp.bfloat16).astype(jnp.float32)
    grad_values = jnp.einsum("hqk,qhd->khd", attention_low, grad_heads).astype(jnp.bfloat16)
    grad_keys = jnp.einsum("hqk,qhd->khd", grad_scores, query_heads).astype(jnp.bfloat16)
    grad_queries = jnp.einsum("hqk,khd->qhd", grad_scores, key_heads).astype(jnp.bfloat16)
    return (context.reshape(TD, INNER), grad_queries.reshape(TD, INNER),
            grad_keys.reshape(KEYS, INNER), grad_values.reshape(KEYS, INNER))


def reference(dec_states, enc_states, w_query, w_key, w_value, passage_slot, ctx_grad):
    key_index = build_index(passage_slot)
    flat_index = key_index.reshape(-1)
    group_width = INNER // N_DEC
    contexts = []
    encoding_grads = []
    query_grad = jnp.zeros((D, INNER), jnp.float32)
    for micro_batch in range(MB):
        queries = jnp.dot(dec_states[micro_batch], w_query, preferred_element_type=jnp.float32).astype(jnp.bfloat16)
        keys_all = jnp.dot(enc_states[micro_batch], w_key, preferred_element_type=jnp.float32).astype(jnp.bfloat16)
        values_all = jnp.dot(enc_states[micro_batch], w_value, preferred_element_type=jnp.float32).astype(jnp.bfloat16)
        results = lax.map(question_pass, (queries.reshape(N_ENC, TD, INNER), keys_all[key_index],
                                          values_all[key_index], ctx_grad[micro_batch].reshape(N_ENC, TD, INNER)))
        context, grad_queries, grad_keys, grad_values = results
        contexts.append(context.reshape(DEC_ROWS, INNER))
        query_grad = query_grad + lax.dot_general(dec_states[micro_batch], grad_queries.reshape(DEC_ROWS, INNER),
                                                  (((0,), (0,)), ((), ())), preferred_element_type=jnp.float32)
        key_grads = jnp.zeros((ENC_ROWS, INNER), jnp.bfloat16).at[flat_index].set(grad_keys.reshape(ENC_ROWS, INNER))
        value_grads = jnp.zeros((ENC_ROWS, INNER), jnp.bfloat16).at[flat_index].set(grad_values.reshape(ENC_ROWS, INNER))
        summed = jnp.zeros((ENC_ROWS, D), jnp.float32)
        for head_group in range(N_DEC):
            low = head_group * group_width
            high = low + group_width
            partial_value = jnp.dot(key_grads[:, low:high], w_key[:, low:high].T, preferred_element_type=jnp.float32)
            partial_value = partial_value + jnp.dot(value_grads[:, low:high], w_value[:, low:high].T, preferred_element_type=jnp.float32)
            rounded = lax.optimization_barrier(partial_value.astype(jnp.bfloat16))
            summed = summed + rounded.astype(jnp.float32)
        encoding_grads.append(summed.astype(jnp.bfloat16))
    return (jnp.stack(contexts), query_grad, jnp.stack(encoding_grads))
```

```python
import jax
import jax.numpy as jnp
from jax import lax
from jax.experimental import pallas as pl
from jax.experimental.pallas import tpu as pltpu
from jax.sharding import Mesh, PartitionSpec as P

HEAD_DIM = 64
SCALE = 0.125
LOW = jnp.bfloat16
WIDE = jnp.float32
AXES = ("x", "yh", "z", "yl", "core")
SIZES = (4, 4, 8, 2, 2)
ENC = ("x", "yh", "z")
PLANE = ("yh", "z")
DEC = ("yl", "core")
GROUP = 256


def exchange(x, axis):
    return lax.all_to_all(x, axis, split_axis=0, concat_axis=0, tiled=True)


def spread(x, axis, size):
    return exchange(jnp.broadcast_to(x[None], (size,) + x.shape), axis)


def passed_along(x, by):
    size = SIZES[0] * SIZES[1] * SIZES[2]
    return lax.ppermute(x, ENC, [(i, (i + by) % size) for i in range(size)])


def dot(a, b, contract):
    return lax.dot_general(a, b, ((contract[:1], contract[1:]), ((), ())), preferred_element_type=WIDE)


def attention_kernel(q_ref, kv_ref, grad_ref, ctx_ref, gq_ref, gkv_ref):
    rows, width = q_ref.shape
    batches = 2
    queries = rows // batches
    keys = kv_ref.shape[0] // batches
    heads = GROUP // HEAD_DIM
    row_head = lax.broadcasted_iota(jnp.int32, (heads * queries, GROUP), 0) // queries
    col_head = lax.broadcasted_iota(jnp.int32, (heads * queries, GROUP), 1) // HEAD_DIM
    own = row_head == col_head
    col_small = lax.broadcasted_iota(jnp.int32, (queries, GROUP), 1) // HEAD_DIM

    def per_head(x):
        return jnp.where(own, jnp.concatenate([x] * heads, axis=0), jnp.zeros((), x.dtype))

    def merged(x):
        out = x[:queries]
        for h in range(1, heads):
            out = jnp.where(col_small == h, x[h * queries : (h + 1) * queries], out)
        return out

    for b in range(batches):
        for g in range(width // GROUP):
            qs, ks = pl.ds(b * queries, queries), pl.ds(b * keys, keys)
            cs, vs = pl.ds(g * GROUP, GROUP), pl.ds(width + g * GROUP, GROUP)
            query = per_head(q_ref[qs, cs])
            grad = per_head(grad_ref[qs, cs])
            key, value = kv_ref[ks, cs], kv_ref[ks, vs]
            scores = dot(query, key, (1, 1)) * SCALE
            raw = jnp.exp(scores - jnp.max(scores, axis=-1, keepdims=True))
            attention = raw / jnp.sum(raw, axis=-1, keepdims=True)
            low = attention.astype(LOW)
            ctx_ref[qs, cs] = merged(dot(low, value, (1, 0))).astype(LOW)
            grad_attention = dot(grad, value, (1, 1))
            correction = jnp.sum(attention * grad_attention, axis=-1, keepdims=True)
            grad_scores = (attention * (grad_attention - correction) * SCALE).astype(LOW)
            gkv_ref[ks, vs] = dot(low, grad, (0, 0)).astype(LOW)
            gkv_ref[ks, cs] = dot(grad_scores, query, (0, 0)).astype(LOW)
            gq_ref[qs, cs] = merged(dot(grad_scores, key, (1, 0))).astype(LOW)


def attention_pass(q, kv, grad):
    whole = pl.BlockSpec(memory_space=pltpu.VMEM)
    return pl.pallas_call(
        attention_kernel,
        out_shape=(
            jax.ShapeDtypeStruct(q.shape, LOW),
            jax.ShapeDtypeStruct(q.shape, LOW),
            jax.ShapeDtypeStruct(kv.shape, LOW),
        ),
        in_specs=[whole] * 3,
        out_specs=(whole,) * 3,
        compiler_params=pltpu.CompilerParams(vmem_limit_bytes=24 * 1024 * 1024),
        cost_estimate=pl.CostEstimate(flops=940_000_000, bytes_accessed=3 << 20, transcendentals=1 << 18),
    )(q, kv, grad)


def on_device(dec_states, enc_states, w_query, w_key, w_value, passage_slot, ctx_grad):
    batches, dec_rows, model = dec_states.shape
    enc_rows = enc_states.shape[1]
    width = w_query.shape[1]
    passages = passage_slot.shape[1]
    length = enc_rows // passages
    half = length // 2
    quarter = model // 4
    dec_flat = dec_states.reshape(batches * dec_rows, model)
    yl, core = lax.axis_index("yl"), lax.axis_index("core")
    order = passage_slot[0]
    positions = jnp.arange(passages, dtype=jnp.int32)
    inverse = jnp.sum(positions[:, None] * (order[:, None] == positions[None, :]).astype(jnp.int32), axis=0)

    by_slot = enc_states.reshape(batches, passages, length, model)
    own_part = lax.dynamic_index_in_dim(by_slot, core, 0, False)
    own_part = lax.dynamic_slice_in_dim(own_part, yl * half, half, 1)
    parts = jnp.stack(
        [passed_along(lax.dynamic_index_in_dim(own_part, order[j], 0, False), -j) for j in range(1, passages)]
    )
    parts = lax.all_gather(parts, DEC, axis=0, tiled=False)
    parts = parts.reshape(2, 2, passages - 1, half, model)
    parts = jnp.transpose(parts, (1, 2, 0, 3, 4)).reshape(batches, passages - 1, length, model)
    near = lax.dynamic_index_in_dim(by_slot, order[0], 1, True)
    enc_flat = jnp.concatenate([near, parts], axis=1).reshape(batches * enc_rows, model)

    weights = spread(jnp.concatenate([w_key, w_value, w_query], axis=1), PLANE, 32).reshape(quarter, 3 * width)
    weight_kv = spread(weights[:, : 2 * width], "x", 4).reshape(model, 2 * width)
    weight_q = weights[:, 2 * width :]

    dec_quarter = dec_flat.reshape(batches * dec_rows, 4, quarter)
    dec_quarter = exchange(jnp.transpose(dec_quarter, (1, 0, 2)), "x").reshape(4 * batches * dec_rows, quarter)
    q_parts = dot(dec_quarter, weight_q, (1, 0)).reshape(4, batches * dec_rows, width)
    queries = jnp.sum(exchange(q_parts, "x"), axis=0).astype(LOW)

    kv = dot(enc_flat, weight_kv, (1, 0)).astype(LOW)
    context, grad_queries, grad_kv = attention_pass(queries, kv, ctx_grad.reshape(batches * dec_rows, width))

    partial = dot(grad_kv, weight_kv, (1, 1)).astype(LOW).reshape(batches, passages, 2, half, model)
    partial = jnp.transpose(partial, (2, 0, 1, 3, 4)).reshape(4, passages, half, model)
    received = exchange(partial, DEC)
    summed = jnp.sum(received.astype(WIDE), axis=0).astype(LOW)
    back = jnp.stack([summed[0]] + [passed_along(summed[j], j) for j in range(1, passages)])
    back = jnp.take(back, inverse, axis=0)
    back = lax.all_gather(back, DEC, axis=0, tiled=False).reshape(2, 2, passages, half, model)
    grad_enc = jnp.transpose(back, (1, 2, 0, 3, 4)).reshape(batches, enc_rows, model)

    gq = spread(grad_queries, "x", 4).reshape(4 * batches * dec_rows, width)
    share = dot(dec_quarter, gq, (0, 0)).astype(LOW).reshape(32, quarter // 32, width)
    grad_query = jnp.sum(exchange(share, PLANE).astype(WIDE), axis=0)
    return context.reshape(batches, dec_rows, width), grad_query, grad_enc


def solution(mesh):
    fine = Mesh(mesh.devices.reshape(SIZES), AXES)
    in_specs = (
        P(None, ENC, None),
        P(None, ENC, None),
        P(ENC, DEC),
        P(ENC, DEC),
        P(ENC, DEC),
        P(ENC, None),
        P(None, ENC, DEC),
    )
    out_specs = (P(None, ENC, DEC), P(ENC, DEC), P(None, ENC, None))
    return jax.shard_map(on_device, mesh=fine, in_specs=in_specs, out_specs=out_specs, check_vma=False)
```

```python
import jax
import jax.numpy as jnp
from jax import lax
from jax.experimental import pallas as pl
from jax.experimental.pallas import tpu as pltpu
from jax.sharding import Mesh, PartitionSpec as P

HEAD_DIM = 64
SCALE = 0.125
LOW = jnp.bfloat16
WIDE = jnp.float32
AXES = ("x", "yh", "z", "yl", "core")
SIZES = (4, 4, 8, 2, 2)
ENC = ("x", "yh", "z")
PLANE = ("yh", "z")
DEC = ("yl", "core")
GROUP = 256
MIB = 1024 * 1024
VMEM = pl.BlockSpec(memory_space=pltpu.VMEM)
SMEM = pl.BlockSpec(memory_space=pltpu.SMEM)
ANY = pl.BlockSpec(memory_space=pl.ANY)


def exchange(x, axis):
    return lax.all_to_all(x, axis, split_axis=0, concat_axis=0, tiled=True)


def spread(x, axis, size):
    return exchange(jnp.broadcast_to(x[None], (size,) + x.shape), axis)


def shifted(x, axis, by):
    size = 1
    for name in (axis,) if isinstance(axis, str) else axis:
        size *= SIZES[AXES.index(name)]
    return lax.ppermute(x, axis, [(i, (i + by) % size) for i in range(size)])


def dot(a, b, contract):
    return lax.dot_general(a, b, ((contract[:1], contract[1:]), ((), ())), preferred_element_type=WIDE)


def call(kernel, out, ins, specs, out_specs, flops=0, moved=1 << 20, scratch=(), limit=16):
    return pl.pallas_call(
        kernel,
        out_shape=out,
        in_specs=specs,
        out_specs=out_specs,
        scratch_shapes=scratch,
        compiler_params=pltpu.CompilerParams(vmem_limit_bytes=limit * MIB),
        cost_estimate=pl.CostEstimate(flops=flops, bytes_accessed=moved, transcendentals=0),
    )(*ins)


X, YL, CORE = 4, 5, 6


def passages_kernel(scalar, enc_ref, own_ref, near_ref, own_other_ref, near_other_ref, out_ref):
    keys = enc_ref.shape[1]
    length = keys // 4
    half = length // 2
    quarter = out_ref.shape[2]
    yl, core = scalar[YL], scalar[CORE]
    first = pl.multiple_of(scalar[0] * length, length)
    parts = ((own_ref, core, yl), (near_ref, core, 1 - yl), (own_other_ref, 1 - core, yl), (near_other_ref, 1 - core, 1 - yl))
    for k in range(4):
        columns = pl.ds(pl.multiple_of(lax.rem(scalar[X] + k, 4) * quarter, quarter), quarter)
        for b in range(2):
            out_ref[k, pl.ds(b * keys, length), :] = enc_ref[b, pl.ds(first, length), columns]
        for part, b, place in parts:
            for j in range(1, 4):
                rows = pl.multiple_of(b * keys + j * length + place * half, half)
                out_ref[k, pl.ds(rows, half), :] = part[j - 1, :, columns]


def attention_kernel(q_ref, kv_ref, grad_ref, ctx_ref, gq_ref, gkv_ref):
    rows, width = q_ref.shape
    batches = 2
    queries = rows // batches
    keys = kv_ref.shape[0] // batches
    heads = GROUP // HEAD_DIM
    row_head = lax.broadcasted_iota(jnp.int32, (heads * queries, GROUP), 0) // queries
    col_head = lax.broadcasted_iota(jnp.int32, (heads * queries, GROUP), 1) // HEAD_DIM
    own = row_head == col_head
    col_small = lax.broadcasted_iota(jnp.int32, (queries, GROUP), 1) // HEAD_DIM

    def per_head(x):
        return jnp.where(own, jnp.concatenate([x] * heads, axis=0), jnp.zeros((), x.dtype))

    def merged(x):
        out = x[:queries]
        for h in range(1, heads):
            out = jnp.where(col_small == h, x[h * queries : (h + 1) * queries], out)
        return out

    for b in range(batches):
        for g in range(width // GROUP):
            qs, ks = pl.ds(b * queries, queries), pl.ds(b * keys, keys)
            cs, vs = pl.ds(g * GROUP, GROUP), pl.ds(width + g * GROUP, GROUP)
            query = per_head(q_ref[qs, cs])
            grad = per_head(grad_ref[qs, cs])
            key, value = kv_ref[ks, cs], kv_ref[ks, vs]
            scores = dot(query, key, (1, 1)) * SCALE
            raw = jnp.exp(scores - jnp.max(scores, axis=-1, keepdims=True))
            attention = raw / jnp.sum(raw, axis=-1, keepdims=True)
            low = attention.astype(LOW)
            ctx_ref[qs, cs] = merged(dot(low, value, (1, 0))).astype(LOW)
            grad_attention = dot(grad, value, (1, 1))
            correction = jnp.sum(attention * grad_attention, axis=-1, keepdims=True)
            grad_scores = (attention * (grad_attention - correction) * SCALE).astype(LOW)
            gkv_ref[ks, vs] = dot(low, grad, (0, 0)).astype(LOW)
            gkv_ref[ks, cs] = dot(grad_scores, query, (0, 0)).astype(LOW)
            gq_ref[qs, cs] = merged(dot(grad_scores, key, (1, 0))).astype(LOW)


def partial_kernel(other, scalar, grad_ref, *refs):
    out_ref = refs[-1]
    rows = out_ref.shape[0]
    batch = 1 - scalar[CORE] if other else scalar[CORE]
    grad = grad_ref[pl.ds(pl.multiple_of(batch * rows, rows), rows), :]
    quarter = out_ref.shape[1] // 4
    for (k, offset), weight in zip(PIECES, refs):
        start = pl.multiple_of(lax.rem(scalar[X] + k, 4) * quarter + offset, 256)
        out_ref[:, pl.ds(start, weight.shape[0])] = dot(grad, weight[...], (1, 1)).astype(LOW)


def place_kernel(scalar, *refs):
    parts, out_ref, sems = refs[:4], refs[4], refs[5]
    half = parts[0].shape[1]
    copies = []
    for i, part in enumerate(parts):
        b = scalar[CORE] if i < 2 else 1 - scalar[CORE]
        place = scalar[YL] if i % 2 == 0 else 1 - scalar[YL]
        for j in range(4):
            rows = pl.multiple_of(scalar[j] * 2 * half + place * half, half)
            copy = pltpu.make_async_copy(part.at[j], out_ref.at[b, pl.ds(rows, half)], sems.at[len(copies)])
            copy.start()
            copies.append(copy)
    for copy in copies:
        copy.wait()


PIECES = ((0, 0), (1, 0), (3, 0), (2, 0), (2, 256))


def around(own):
    above = shifted(own, "x", -1)
    below = shifted(own, "x", 1)
    size = own.shape[0] // 2
    return [own, above, below, shifted(above[:size], "x", -1), shifted(below[size:], "x", 1)]


def project(quarters, pieces):
    total = None
    for (k, offset), piece in zip(PIECES, pieces):
        term = dot(quarters[k][:, offset : offset + piece.shape[0]], piece, (1, 0))
        total = term if total is None else total + term
    return total.astype(LOW)


def on_device(dec_states, enc_states, w_query, w_key, w_value, passage_slot, ctx_grad):
    batches, dec_rows, model = dec_states.shape
    enc_rows = enc_states.shape[1]
    width = w_query.shape[1]
    passages = passage_slot.shape[1]
    length = enc_rows // passages
    half = length // 2
    quarter = model // 4
    rows = batches * dec_rows
    dec_flat = dec_states.reshape(rows, model)
    x, yl, core = lax.axis_index("x"), lax.axis_index("yl"), lax.axis_index("core")
    order = passage_slot[0]
    scalar = jnp.concatenate([order, jnp.stack([x, yl, core, x]).astype(jnp.int32)])
    low = lambda *shape: jax.ShapeDtypeStruct(shape, LOW)

    by_slot = enc_states.reshape(batches, passages, length, model)
    fetched = []
    for j in range(1, passages):
        piece = lax.dynamic_slice(by_slot, (core, order[j], yl * half, 0), (1, 1, half, model))
        fetched.append(shifted(piece.reshape(half, model), ENC, -j))
    dec_parts = []
    for k in range(4):
        part = lax.dynamic_slice_in_dim(dec_flat, ((x + k) % 4) * quarter, quarter, 1)
        dec_parts.append(shifted(part, "x", k) if k else part)
    weights = spread(jnp.concatenate([w_key, w_value, w_query], axis=1), PLANE, 32).reshape(quarter, 3 * width)
    fetched, dec_parts, weights = lax.optimization_barrier((fetched, dec_parts, weights))
    pieces = around(weights[:, : 2 * width])
    dec_quarter = jnp.take(jnp.stack(dec_parts), (x - jnp.arange(4)) % 4, axis=0).reshape(4 * rows, quarter)
    queries = dot(dec_quarter, weights[:, 2 * width :], (1, 0)).reshape(4, rows, width)
    queries = jnp.sum(exchange(queries, "x"), axis=0).astype(LOW)
    own = jnp.stack(fetched)
    near = shifted(own, "yl", 1)
    quarters = call(
        passages_kernel,
        low(4, batches * enc_rows, quarter),
        (scalar, enc_states, own, near, shifted(own, "core", 1), shifted(near, "core", 1)),
        [SMEM] + [VMEM] * 5,
        VMEM,
        moved=4 * MIB,
    )
    kv = project(quarters, pieces)

    context, gq, gkv = call(
        attention_kernel,
        (low(rows, width), low(rows, width), low(*kv.shape)),
        (queries, kv, ctx_grad.reshape(rows, width)),
        [VMEM] * 3,
        (VMEM,) * 3,
        flops=940_000_000,
        moved=3 * MIB,
    )

    def partial(other):
        def kernel(*refs):
            partial_kernel(other, *refs)

        return call(
            kernel,
            low(enc_rows, model),
            (scalar, gkv, *pieces),
            [SMEM] + [VMEM] * 6,
            VMEM,
            flops=1_080_000_000,
            moved=6 * MIB,
        )

    got = shifted(partial(True), "core", 1)
    total = (partial(False).astype(WIDE) + got.astype(WIDE)).astype(LOW).reshape(passages, 2, half, model)
    gq_parts = spread(gq, "x", 4).reshape(4 * rows, width)
    total, gq_parts = lax.optimization_barrier((total, gq_parts))
    got = shifted(lax.dynamic_index_in_dim(total, 1 - yl, 1, False), "yl", 1)
    total = lax.dynamic_index_in_dim(total, yl, 1, False).astype(WIDE) + got.astype(WIDE)
    total = total.astype(LOW)
    back = jnp.stack([shifted(total[j], ENC, j) if j else total[j] for j in range(passages)])
    near = shifted(back, "yl", 1)
    grad_enc = call(
        place_kernel,
        low(batches, enc_rows, model),
        (scalar, back, near, shifted(back, "core", 1), shifted(near, "core", 1)),
        [SMEM] + [ANY] * 4,
        ANY,
        moved=4 * MIB,
        scratch=[pltpu.SemaphoreType.DMA((16,))],
    )

    share = dot(dec_quarter, gq_parts, (0, 0)).astype(LOW).reshape(32, quarter // 32, width)
    grad_query = jnp.sum(exchange(share, PLANE).astype(WIDE), axis=0)
    return context.reshape(batches, dec_rows, width), grad_query, grad_enc


def solution(mesh):
    fine = Mesh(mesh.devices.reshape(SIZES), AXES)
    in_specs = (
        P(None, ENC, None),
        P(None, ENC, None),
        P(ENC, DEC),
        P(ENC, DEC),
        P(ENC, DEC),
        P(ENC, None),
        P(None, ENC, DEC),
    )
    out_specs = (P(None, ENC, DEC), P(ENC, DEC), P(None, ENC, None))
    return jax.shard_map(on_device, mesh=fine, in_specs=in_specs, out_specs=out_specs, check_vma=False)
```
